32 devices in a mesh: tm: 8 (over z, core), space: 4 (over y, x).
Axes of the slice: x: 2, y: 2, z: 4, core: 2. Of those that a mesh axis runs over, the one named last changes fastest.
Arguments:
- queries: bfloat16 [8, 512, 48, 128], P('tm', 'space'), may hold values from -14 to 14
- noisy_keys: bfloat16 [8, 512, 48, 128], P('tm', 'space'), may hold values from -14 to 14
- noisy_values: bfloat16 [8, 512, 48, 128], P('tm', 'space'), may hold values from -6 to 6
- cache_keys: bfloat16 [8, 512, 48, 128], P('tm', 'space'), may hold values from -12 to 12
- cache_values: bfloat16 [8, 512, 48, 128], P('tm', 'space'), may hold values from -6 to 6
- block_list: int32 [8, 4, 12], P('tm'), may hold values from 0 to 15, as said below
- block_count: int32 [8, 4], P('tm'), may hold values from 1 to 12
- valid_tokens: int32 [8], replicated, may hold values from 385 to 512
Outputs:
- attended: bfloat16 [8, 512, 48, 128], P('tm', 'space')
The draws below stay inside these ranges and needn't reach their ends.
Inputs may be any that keep to these rules, and one draw needn't show every extreme that they name: `block_list`: entries index the 16 key blocks of stretch c's window in order of offset, the last 4 being stretch c's own blocks. The first block_count[c, a] entries are distinct and name only blocks of stretches 0 or later; the first of them is query block a's own block; later entries repeat that own block.
All inputs are finite; a program needn't handle non-finite values.
Results may differ from the reference program's by a relative error of at most 0.0035.
Values may be sent and summed in bfloat16 or wider, within the bound.
A program may use at most 128 MiB of HBM per device.

```python
import math
import jax
import jax.numpy as jnp
from jax import lax

HEADS = 48
D_HEAD = 128
BLOCK = 128
WIN = 4
LIST = 12
STRETCHES = 8
STRETCH = 512


def drawn_pair(key):
    shape = (STRETCHES, STRETCH, HEADS, D_HEAD)
    key_seed = jax.random.fold_in(key, 11)
    query_seed = jax.random.fold_in(key, 12)
    key_draw = jnp.clip(2.0 * jax.random.normal(key_seed, shape, jnp.float32), -14.0, 14.0)
    query_draw = jnp.clip(jax.random.normal(query_seed, shape, jnp.float32), -6.0, 6.0)
    return (query_draw, key_draw)


def draw_queries(key, part):
    return drawn_pair(key)[0].astype(jnp.bfloat16)


def draw_noisy_keys(key, part):
    return drawn_pair(key)[1].astype(jnp.bfloat16)


def permuted_row(row_seed):
    return jax.random.permutation(row_seed, WIN * (STRETCH // BLOCK))


def visible_lists(key):
    base_seed = jax.random.fold_in(key, 31)
    block_total = STRETCH // BLOCK
    span = WIN * block_total
    row_seeds = jax.random.split(jax.random.fold_in(base_seed, 1), STRETCHES * block_total)
    priority = jax.vmap(permuted_row)(row_seeds).reshape(STRETCHES, block_total, span).astype(jnp.int32)
    stretch_ids = jnp.arange(STRETCHES)[:, None, None]
    query_ids = jnp.arange(block_total)[None, :, None]
    candidate = jnp.arange(span)[None, None, :]
    first_offset = jnp.maximum(WIN - 1 - stretch_ids, 0)
    usable = candidate // block_total >= first_offset
    own_block = candidate == (WIN - 1) * block_total + query_ids
    forced_row = (stretch_ids == STRETCHES - 1) & (query_ids == 0)
    priority = jnp.where(forced_row & (candidate == 0), -2, priority)
    priority = jnp.where(forced_row & (candidate == span - 1), -1, priority)
    priority = jnp.where(own_block, -3, priority)
    ranking = priority + jnp.where(usable, 0, 4 * span)
    ordering = jnp.argsort(ranking, axis=-1, stable=True)
    usable_count = (WIN - first_offset[:, :, 0]) * block_total
    stretch_cap = jax.random.randint(jax.random.fold_in(base_seed, 2), (STRETCHES, 1), max(LIST // 4, 1), LIST + 1)
    stretch_cap = jnp.where(stretch_ids[:, :, 0] == STRETCHES - 1, LIST, stretch_cap)
    upper = jnp.minimum(stretch_cap, usable_count)
    counts_drawn = jax.random.randint(jax.random.fold_in(base_seed, 3), (STRETCHES, block_total), 1, upper + 1)
    counts_drawn = jnp.where(forced_row[:, :, 0], LIST, counts_drawn)
    entries = ordering[:, :, :LIST]
    slot_ids = jnp.arange(LIST)[None, None, :]
    own_index = (WIN - 1) * block_total + query_ids
    entries = jnp.where(slot_ids < counts_drawn[:, :, None], entries, own_index)
    return (entries.astype(jnp.int32), counts_drawn.astype(jnp.int32))


def draw_block_list(key, part):
    return visible_lists(key)[0]


def draw_block_count(key, part):
    return visible_lists(key)[1]


def with_ends(values, stream_key, least, top_value):
    spot = [jax.random.randint(jax.random.fold_in(stream_key, axis), (), 0, length) for axis, length in enumerate(values.shape)]
    widest = values.shape.index(max(values.shape))
    beside = spot[:widest] + [(spot[widest] + 1) % values.shape[widest]] + spot[widest + 1:]
    return values.at[tuple(spot)].set(least).at[tuple(beside)].set(top_value)


def shard_levels(rng, shape, cuts, smallest, high):
    factor_of, own = 1.0, jax.random.fold_in(rng, 6)
    for position, parts in cuts:
        steps = jnp.exp(jax.random.uniform(jax.random.fold_in(own, position), (parts,), jnp.float32, smallest / len(cuts), high / len(cuts)))
        factor_of = factor_of * jnp.repeat(steps, shape[position] // parts).reshape([-1 if axis == position else 1 for axis in range(len(shape))])
    return factor_of


def bell_draw(stream_key, dims, deviation, limit, pieces=(), held_as=jnp.bfloat16):
    drawn = jax.random.normal(stream_key, dims, jnp.float32) * deviation
    if len(pieces) > 0:
        drawn = shard_levels(stream_key, dims, pieces, -0.22, 0.18) * drawn
    return jnp.clip(drawn, min=-limit, max=limit).astype(held_as)


def setup_inputs(seed: int = 0) -> dict:
    keys = jax.random.split(jax.random.key(seed), 9)
    queries = draw_queries(jax.random.fold_in(keys[8], 71), 0)
    noisy_keys = draw_noisy_keys(jax.random.fold_in(keys[8], 71), 0)
    noisy_values = bell_draw(keys[2], (STRETCHES, STRETCH, HEADS, D_HEAD), 1.0, 6.0, ((0, 8), (1, 4)))
    cache_keys = bell_draw(keys[3], (STRETCHES, STRETCH, HEADS, D_HEAD), 2.0, 12.0, ((0, 8), (1, 4)))
    cache_values = bell_draw(keys[4], (STRETCHES, STRETCH, HEADS, D_HEAD), 1.0, 6.0, ((0, 8), (1, 4)))
    block_list = draw_block_list(jax.random.fold_in(keys[8], 71), 0)
    block_count = draw_block_count(jax.random.fold_in(keys[8], 71), 0)
    valid_tokens = with_ends(jax.random.randint(keys[7], (STRETCHES,), STRETCH - BLOCK + 1, STRETCH + 1), jax.random.fold_in(keys[7], 1), STRETCH - BLOCK + 1, STRETCH).astype(jnp.int32)
    return {"queries": queries, "noisy_keys": noisy_keys, "noisy_values": noisy_values, "cache_keys": cache_keys, "cache_values": cache_values, "block_list": block_list, "block_count": block_count, "valid_tokens": valid_tokens}


NEG = -1e+30

def one_stretch(stretch_now, queries, noisy_keys, noisy_values, cache_keys, cache_values, block_list, block_count, valid_tokens):
    positions = jnp.arange(STRETCH).astype(jnp.int32)
    key_parts = []
    value_parts = []
    live_parts = []
    for offset in range(WIN):
        source_stretch = stretch_now - (WIN - 1) + offset
        safe_source = jnp.maximum(source_stretch, 0).astype(jnp.int32)
        if offset == WIN - 1:
            key_parts.append(noisy_keys[stretch_now])
            value_parts.append(noisy_values[stretch_now])
        else:
            key_parts.append(cache_keys[safe_source])
            value_parts.append(cache_values[safe_source])
        live_parts.append((source_stretch >= 0) & (positions < valid_tokens[safe_source]))
    window_keys = jnp.concatenate(key_parts, 0)
    window_values = jnp.concatenate(value_parts, 0)
    key_live = jnp.concatenate(live_parts, 0)
    block_total = STRETCH // BLOCK
    stretch_lists = block_list[stretch_now]
    stretch_counts = block_count[stretch_now]
    entry_live = jnp.arange(LIST).astype(jnp.int32)[None, :] < stretch_counts[:, None]
    candidates = jnp.arange(WIN * block_total).astype(jnp.int32)
    block_seen = jnp.any((stretch_lists[:, :, None] == candidates[None, None, :]) & entry_live[:, :, None], axis=1)
    token_seen = jnp.repeat(jnp.repeat(block_seen, BLOCK, 0), BLOCK, 1) & key_live[None, :]
    query_live = positions < valid_tokens[stretch_now]
    score_scale = 1.0 / math.sqrt(D_HEAD)

    def one_head(operands):
        query_rows, key_rows, value_rows = operands
        scores = jnp.dot(query_rows, key_rows.T, preferred_element_type=jnp.float32) * score_scale
        scores = jnp.where(token_seen, scores, NEG)
        row_best = lax.optimization_barrier(jnp.max(scores, axis=1, keepdims=True))
        weights = jnp.where(token_seen, jnp.exp(scores - row_best), 0.0)
        row_total = lax.optimization_barrier(jnp.sum(weights, axis=1, keepdims=True))
        mixed_rows = jnp.dot(weights.astype(jnp.bfloat16), value_rows, preferred_element_type=jnp.float32) / row_total
        return jnp.where(query_live[:, None], mixed_rows, 0.0).astype(jnp.bfloat16)
    result = lax.map(one_head, (jnp.moveaxis(queries[stretch_now], 1, 0), jnp.moveaxis(window_keys, 1, 0), jnp.moveaxis(window_values, 1, 0)))
    return jnp.moveaxis(result, 0, 1)

def reference(queries, noisy_keys, noisy_values, cache_keys, cache_values, block_list, block_count, valid_tokens):

    def per_stretch(stretch_now):
        return one_stretch(stretch_now, queries, noisy_keys, noisy_values, cache_keys, cache_values, block_list, block_count, valid_tokens)
    return lax.map(per_stretch, jnp.arange(STRETCHES).astype(jnp.int32))
```

```python
import functools
import math

import jax
import jax.numpy as jnp
from jax import lax
from jax.experimental import pallas as pl
from jax.experimental.pallas import tpu as pltpu
from jax.sharding import PartitionSpec as P

BLOCK = 128
WIN = 4
NEG = -1e30


def window_bias(stretch_now, stretch_len, block_list, block_count, valid_tokens):
    blocks = stretch_len // BLOCK
    slots = jnp.arange(block_list.shape[1])
    used = slots[None, :] < block_count[:, None]
    window_blocks = jnp.arange(WIN * blocks)
    seen = jnp.any(
        (block_list[:, :, None] == window_blocks[None, None, :]) & used[:, :, None], axis=1
    )
    stretches = jnp.arange(valid_tokens.shape[0])
    sources = stretch_now - (WIN - 1) + jnp.arange(WIN)
    lengths = jnp.sum(
        jnp.where(sources[:, None] == stretches[None, :], valid_tokens[None, :], 0), axis=1
    )
    live = (jnp.arange(stretch_len)[None, :] < lengths[:, None]).reshape(-1)
    token_seen = jnp.repeat(seen, BLOCK, axis=1) & live[None, :]
    own = jnp.sum(jnp.where(stretches == stretch_now, valid_tokens, 0))
    row_live = (jnp.arange(stretch_len) < own).astype(jnp.float32)
    bias = jnp.where(token_seen, 0.0, NEG).astype(jnp.float32)
    return bias[:, None, :], row_live[:, None]


def attend(q, k_parts, v_parts, bias, row_live, fold):
    rows = q.shape[0]
    scores = []
    start = 0
    best = None
    for k in k_parts:
        width = k.shape[0]
        s = lax.dot_general(
            q, k, (((1,), (1,)), ((), ())), preferred_element_type=jnp.float32
        )
        s = s.reshape(rows // BLOCK, BLOCK, width) + bias[:, :, start : start + width]
        s = s.reshape(rows, width)
        top = jnp.max(s, axis=1, keepdims=True)
        best = top if best is None else jnp.maximum(best, top)
        scores.append(s)
        start += width
    shift = best * fold
    total = None
    out = None
    for s, v in zip(scores, v_parts):
        w = jnp.exp2(s * fold - shift)
        part = jnp.sum(w, axis=1, keepdims=True)
        o = jnp.dot(w.astype(jnp.bfloat16), v, preferred_element_type=jnp.float32)
        total = part if total is None else total + part
        out = o if out is None else out + o
    return jnp.where(row_live > 0, out / total, 0.0).astype(jnp.bfloat16)


def rows_at_once(stretch_len):
    return BLOCK * max(1, min(stretch_len // BLOCK, (1 << 20) // (WIN * stretch_len * BLOCK)))


def attention_kernel(fold, rows, q_ref, k_ref, v_ref, pk_ref, pv_ref, bias_ref, live_ref, o_ref):
    stretch_len = q_ref.shape[1]
    blocks = rows // BLOCK

    def step(i, carry):
        at = pl.multiple_of(i * rows, rows)
        k_parts = [pk_ref[o, 0] for o in range(WIN - 1)] + [k_ref[0]]
        v_parts = [pv_ref[o, 0] for o in range(WIN - 1)] + [v_ref[0]]
        o_ref[0, pl.ds(at, rows)] = attend(
            q_ref[0, pl.ds(at, rows)],
            k_parts,
            v_parts,
            bias_ref[pl.ds(i * blocks, blocks)],
            live_ref[pl.ds(at, rows)],
            fold,
        )
        return carry

    lax.fori_loop(0, stretch_len // rows, step, 0)


def attention(q, k, v, past_k, past_v, bias, row_live):
    heads, stretch_len, d = q.shape
    fold = math.log2(math.e) / math.sqrt(d)
    rows = rows_at_once(stretch_len)
    one = pl.BlockSpec((1, stretch_len, d), lambda h: (h, 0, 0))
    past = pl.BlockSpec((WIN - 1, 1, stretch_len, d), lambda h: (0, h, 0, 0))
    return pl.pallas_call(
        functools.partial(attention_kernel, fold, rows),
        out_shape=jax.ShapeDtypeStruct(q.shape, q.dtype),
        grid=(heads,),
        in_specs=[
            one,
            one,
            one,
            past,
            past,
            pl.BlockSpec(bias.shape, lambda h: (0, 0, 0)),
            pl.BlockSpec(row_live.shape, lambda h: (0, 0)),
        ],
        out_specs=one,
        compiler_params=pltpu.CompilerParams(vmem_limit_bytes=50 * 1024 * 1024),
        cost_estimate=pl.CostEstimate(
            flops=4 * heads * stretch_len * WIN * stretch_len * d,
            bytes_accessed=2 * (2 + 2 * WIN) * q.size,
            transcendentals=heads * stretch_len * WIN * stretch_len,
        ),
    )(q, k, v, past_k, past_v, bias, row_live)


def on_device(
    queries,
    noisy_keys,
    noisy_values,
    cache_keys,
    cache_values,
    block_list,
    block_count,
    valid_tokens,
):
    stretch_now = lax.axis_index("tm")
    space = lax.axis_size("space")
    stretch_len = queries.shape[1] * space

    def by_heads(*arrays):
        return jnp.transpose(jnp.concatenate(arrays, 0), (0, 2, 1, 3))

    def spread(x):
        return lax.all_to_all(x, "space", split_axis=1, concat_axis=2, tiled=True)

    cache = spread(by_heads(cache_keys, cache_values))
    fresh = spread(by_heads(queries, noisy_keys, noisy_values))
    count = lax.axis_size("tm")
    earlier = []
    carried = cache
    for _ in range(1, WIN):
        carried = lax.ppermute(carried, "tm", [(i, i + 1) for i in range(count - 1)])
        earlier.append(carried)
    past = jnp.stack(earlier[::-1], 0)
    bias, row_live = window_bias(
        stretch_now, stretch_len, block_list[0], block_count[0], valid_tokens
    )
    out = attention(fresh[0], fresh[1], fresh[2], past[:, 0], past[:, 1], bias, row_live)
    back = lax.all_to_all(out, "space", split_axis=1, concat_axis=0, tiled=True)
    return jnp.transpose(back, (1, 0, 2))[None]


def solution(mesh):
    placed = (
        P("tm", "space", None, None),
        P("tm", "space", None, None),
        P("tm", "space", None, None),
        P("tm", "space", None, None),
        P("tm", "space", None, None),
        P("tm", None, None),
        P("tm", None),
        P(),
    )
    return jax.shard_map(
        on_device,
        mesh=mesh,
        in_specs=placed,
        out_specs=P("tm", "space", None, None),
        check_vma=False,
    )
```

```python
import functools
import math

import jax
import jax.numpy as jnp
from jax import lax
from jax.experimental import pallas as pl
from jax.experimental.pallas import tpu as pltpu
from jax.sharding import PartitionSpec as P

BLOCK = 128
WIN = 4
NEG = -1e30
GROUPS = 6
MESH = pl.DeviceIdType.MESH


def window_bias(stretch_now, stretch_len, block_list, block_count, valid_tokens):
    blocks = stretch_len // BLOCK
    slots = jnp.arange(block_list.shape[1])
    used = slots[None, :] < block_count[:, None]
    window_blocks = jnp.arange(WIN * blocks)
    seen = jnp.any(
        (block_list[:, :, None] == window_blocks[None, None, :]) & used[:, :, None], axis=1
    )
    stretches = jnp.arange(valid_tokens.shape[0])
    sources = stretch_now - (WIN - 1) + jnp.arange(WIN)
    lengths = jnp.sum(
        jnp.where(sources[:, None] == stretches[None, :], valid_tokens[None, :], 0), axis=1
    )
    live = (jnp.arange(stretch_len)[None, :] < lengths[:, None]).reshape(-1)
    token_seen = jnp.repeat(seen, BLOCK, axis=1) & live[None, :]
    own = jnp.sum(jnp.where(stretches == stretch_now, valid_tokens, 0))
    row_live = (jnp.arange(stretch_len) < own).astype(jnp.float32)
    bias = jnp.where(token_seen, 0.0, NEG).astype(jnp.float32)
    return bias[:, None, :], row_live[:, None]


def attend(q, k_parts, v_parts, bias, row_live, fold):
    rows = q.shape[0]
    scores = []
    start = 0
    best = None
    for k in k_parts:
        width = k.shape[0]
        s = lax.dot_general(
            q, k, (((1,), (1,)), ((), ())), preferred_element_type=jnp.float32
        )
        s = s.reshape(rows // BLOCK, BLOCK, width) + bias[:, :, start : start + width]
        s = s.reshape(rows, width)
        top = jnp.max(s, axis=1, keepdims=True)
        best = top if best is None else jnp.maximum(best, top)
        scores.append(s)
        start += width
    shift = best * fold
    total = None
    out = None
    for s, v in zip(scores, v_parts):
        w = jnp.exp2(s * fold - shift)
        part = jnp.sum(w, axis=1, keepdims=True)
        o = jnp.dot(w.astype(jnp.bfloat16), v, preferred_element_type=jnp.float32)
        total = part if total is None else total + part
        out = o if out is None else out + o
    return jnp.where(row_live > 0, out / total, 0.0).astype(jnp.bfloat16)


def rows_at_once(stretch_len):
    return BLOCK * max(1, min(stretch_len // BLOCK, (1 << 20) // (WIN * stretch_len * BLOCK)))


def exchange_kernel(
    fold,
    rows,
    groups,
    cache_in,
    fresh_in,
    bias_ref,
    live_ref,
    out,
    own,
    past,
    fresh,
    mixed,
    cache_send,
    cache_recv,
    fresh_send,
    fresh_recv,
    out_send,
    out_recv,
    hop_send,
    hop_recv,
    here,
):
    c, last = lax.axis_index("tm"), lax.axis_size("tm") - 1
    s, space = lax.axis_index("space"), lax.axis_size("space")
    tokens = cache_in.shape[2]
    heads, stretch_len = own.shape[1], own.shape[2]
    some = heads // groups
    has_next = c < last
    hops = WIN - 1

    def part(g):
        return pl.ds(g * some, some)

    def held_by(p, g):
        return pl.ds(p * heads + g * some, some)

    def tokens_of(p):
        return pl.ds(pl.multiple_of(p * tokens, tokens), tokens)

    def spread(src, dst, send, recv, g, apart):
        p = lax.rem(s + apart, space)
        return pltpu.make_async_remote_copy(
            src_ref=src.at[:, held_by(p, g)],
            dst_ref=dst.at[:, part(g), tokens_of(s)],
            send_sem=send.at[g, apart - 1],
            recv_sem=recv.at[g, apart - 1],
            device_id={"space": p},
            device_id_type=MESH,
        )

    def kept(src, dst, kind, g):
        return pltpu.make_async_copy(
            src.at[:, held_by(s, g)], dst.at[:, part(g), tokens_of(s)], here.at[kind, g]
        )

    def cache_copies(g):
        return [
            spread(cache_in, own, cache_send, cache_recv, g, apart) for apart in range(1, space)
        ], kept(cache_in, own, 0, g)

    def fresh_copies(g):
        return [
            spread(fresh_in, fresh, fresh_send, fresh_recv, g, apart) for apart in range(1, space)
        ], kept(fresh_in, fresh, 1, g)

    def out_copies(g):
        remote = []
        for apart in range(1, space):
            p = lax.rem(s + apart, space)
            remote.append(
                pltpu.make_async_remote_copy(
                    src_ref=mixed.at[part(g), tokens_of(p)],
                    dst_ref=out.at[held_by(s, g)],
                    send_sem=out_send.at[g, apart - 1],
                    recv_sem=out_recv.at[g, apart - 1],
                    device_id={"space": p},
                    device_id_type=MESH,
                )
            )
        local = pltpu.make_async_copy(
            mixed.at[part(g), tokens_of(s)], out.at[held_by(s, g)], here.at[2, g]
        )
        return remote, local

    def start(copies):
        remote, local = copies
        for copy in remote:
            copy.start()
        local.start()

    def arrive(copies):
        remote, local = copies
        for copy in remote:
            copy.wait_recv()
        local.wait()

    def hop(j, g):
        return pltpu.make_async_remote_copy(
            src_ref=own.at[:, part(g)] if j == 0 else past.at[j - 1, :, part(g)],
            dst_ref=past.at[j, :, part(g)],
            send_sem=hop_send.at[j, g],
            recv_sem=hop_recv.at[j, g],
            device_id={"tm": c + 1},
            device_id_type=MESH,
        )

    barrier = pltpu.get_barrier_semaphore()
    for apart in range(1, space):
        pl.semaphore_signal(
            barrier,
            inc=1,
            device_id={"space": lax.rem(s + apart, space)},
            device_id_type=MESH,
        )

    @pl.when(has_next)
    def _():
        pl.semaphore_signal(barrier, inc=1, device_id={"tm": c + 1}, device_id_type=MESH)

    @pl.when(c > 0)
    def _():
        pl.semaphore_signal(barrier, inc=1, device_id={"tm": c - 1}, device_id_type=MESH)

    pl.semaphore_wait(
        barrier, space - 1 + jnp.where(has_next, 1, 0) + jnp.where(c > 0, 1, 0)
    )

    @pl.when(has_next)
    def _():
        start(cache_copies(0))
        if groups > 1:
            start(cache_copies(1))

    start(fresh_copies(0))

    for j in range(hops):

        @pl.when(c <= j)
        def _(j=j):
            def clear(h, carry):
                for kind in range(2):
                    past[j, kind, h] = jnp.zeros(past.shape[3:], past.dtype)
                return carry

            lax.fori_loop(0, heads, clear, 0)

    @pl.when(has_next)
    def _():
        arrive(cache_copies(0))
        hop(0, 0).start()

    def attend_head(h):
        blocks = rows // BLOCK
        k_parts = [past.at[hops - 1 - o, 0, h] for o in range(hops)] + [fresh.at[1, h]]
        v_parts = [past.at[hops - 1 - o, 1, h] for o in range(hops)] + [fresh.at[2, h]]

        def step(i, carry):
            at = pl.multiple_of(i * rows, rows)
            mixed[h, pl.ds(at, rows)] = attend(
                fresh[0, h, pl.ds(at, rows)],
                [k[...] for k in k_parts],
                [v[...] for v in v_parts],
                bias_ref[pl.ds(i * blocks, blocks)],
                live_ref[pl.ds(at, rows)],
                fold,
            )
            return carry

        lax.fori_loop(0, stretch_len // rows, step, 0)

    def turn(g, carry):
        @pl.when((g + 2 < groups) & has_next)
        def _():
            start(cache_copies(g + 2))

        @pl.when(g + 1 < groups)
        def _():
            start(fresh_copies(g + 1))

        for j in range(hops - 1):

            @pl.when((g < groups) & (c >= j + 1))
            def _(j=j):
                hop(j, g).wait_recv()

            @pl.when((g < groups) & (c >= j + 1) & has_next)
            def _(j=j):
                hop(j + 1, g).start()

        @pl.when((g + 1 < groups) & has_next)
        def _():
            arrive(cache_copies(g + 1))
            hop(0, g + 1).start()

        @pl.when(g > 0)
        def _():
            done = g - 1

            @pl.when(c >= hops)
            def _():
                hop(hops - 1, done).wait_recv()

            arrive(fresh_copies(done))

            def one(i, carry):
                attend_head(done * some + i)
                return carry

            lax.fori_loop(0, some, one, 0)
            start(out_copies(done))

        return carry

    lax.fori_loop(0, groups + 1, turn, 0)

    def finish(g, carry):
        @pl.when(has_next)
        def _():
            for copy in cache_copies(g)[0]:
                copy.wait_send()

        for copy in fresh_copies(g)[0]:
            copy.wait_send()
        for j in range(hops):

            @pl.when(has_next & (c >= j))
            def _(j=j):
                hop(j, g).wait_send()

        remote, local = out_copies(g)
        for copy in remote:
            copy.wait()
        local.wait()
        return carry

    lax.fori_loop(0, groups, finish, 0)


def exchange_and_attend(cache, fresh, bias, row_live):
    space = lax.axis_size("space")
    _, all_heads, tokens, d = fresh.shape
    heads, stretch_len = all_heads // space, tokens * space
    groups = max(n for n in range(1, GROUPS + 1) if heads % n == 0)
    fold = math.log2(math.e) / math.sqrt(d)
    rows = rows_at_once(stretch_len)
    dma = pltpu.SemaphoreType.DMA
    return pl.pallas_call(
        functools.partial(exchange_kernel, fold, rows, groups),
        out_shape=jax.ShapeDtypeStruct((all_heads, tokens, d), fresh.dtype),
        in_specs=[
            pl.BlockSpec(memory_space=pl.ANY),
            pl.BlockSpec(memory_space=pl.ANY),
            pl.BlockSpec(memory_space=pltpu.VMEM),
            pl.BlockSpec(memory_space=pltpu.VMEM),
        ],
        out_specs=pl.BlockSpec(memory_space=pl.ANY),
        scratch_shapes=[
            pltpu.VMEM((2, heads, stretch_len, d), fresh.dtype),
            pltpu.VMEM((WIN - 1, 2, heads, stretch_len, d), fresh.dtype),
            pltpu.VMEM((3, heads, stretch_len, d), fresh.dtype),
            pltpu.VMEM((heads, stretch_len, d), fresh.dtype),
        ]
        + [dma((groups, space - 1))] * 6
        + [dma((WIN - 1, groups))] * 2
        + [dma((3, groups))],
        compiler_params=pltpu.CompilerParams(
            collective_id=0, has_side_effects=True, vmem_limit_bytes=50 * 1024 * 1024
        ),
        cost_estimate=pl.CostEstimate(
            flops=4 * heads * stretch_len * WIN * stretch_len * d,
            bytes_accessed=12 * heads * stretch_len * d,
            transcendentals=heads * stretch_len * WIN * stretch_len,
        ),
    )(cache, fresh, bias, row_live)


def on_device(
    queries,
    noisy_keys,
    noisy_values,
    cache_keys,
    cache_values,
    block_list,
    block_count,
    valid_tokens,
):
    stretch_now = lax.axis_index("tm")
    space = lax.axis_size("space")
    stretch_len = queries.shape[1] * space

    def by_heads(*arrays):
        return jnp.transpose(jnp.concatenate(arrays, 0), (0, 2, 1, 3))

    bias, row_live = window_bias(
        stretch_now, stretch_len, block_list[0], block_count[0], valid_tokens
    )
    back = exchange_and_attend(
        by_heads(cache_keys, cache_values),
        by_heads(queries, noisy_keys, noisy_values),
        bias,
        row_live,
    )
    return jnp.transpose(back, (1, 0, 2))[None]


def solution(mesh):
    placed = (
        P("tm", "space", None, None),
        P("tm", "space", None, None),
        P("tm", "space", None, None),
        P("tm", "space", None, None),
        P("tm", "space", None, None),
        P("tm", None, None),
        P("tm", None),
        P(),
    )
    return jax.shard_map(
        on_device,
        mesh=mesh,
        in_specs=placed,
        out_specs=P("tm", "space", None, None),
        check_vma=False,
    )
```

```python
import functools
import math

import jax
import jax.numpy as jnp
from jax import lax
from jax.experimental import pallas as pl
from jax.experimental.pallas import tpu as pltpu
from jax.sharding import PartitionSpec as P

BLOCK = 128
WIN = 4
NEG = -1e30
GROUPS = 12
MESH = pl.DeviceIdType.MESH


def attend(q, k_parts, v_parts, bias, row_live, fold):
    rows = q.shape[0]
    scores = []
    start = 0
    best = None
    for k in k_parts:
        width = k.shape[0]
        s = lax.dot_general(
            q, k, (((1,), (1,)), ((), ())), preferred_element_type=jnp.float32
        )
        s = s.reshape(rows // BLOCK, BLOCK, width) + bias[:, :, start : start + width]
        s = s.reshape(rows, width)
        top = jnp.max(s, axis=1, keepdims=True)
        best = top if best is None else jnp.maximum(best, top)
        scores.append(s)
        start += width
    shift = best * fold
    total = None
    out = None
    for s, v in zip(scores, v_parts):
        w = jnp.exp2(s * fold - shift)
        part = jnp.sum(w, axis=1, keepdims=True)
        o = jnp.dot(w.astype(jnp.bfloat16), v, preferred_element_type=jnp.float32)
        total = part if total is None else total + part
        out = o if out is None else out + o
    return jnp.where(row_live, out / total, 0.0).astype(jnp.bfloat16)


def rows_at_once(stretch_len):
    return BLOCK * max(1, min(stretch_len // BLOCK, (1 << 20) // (WIN * stretch_len * BLOCK)))


def exchange_kernel(
    fold,
    rows,
    groups,
    ck_in,
    cv_in,
    q_in,
    k_in,
    v_in,
    list_ref,
    count_ref,
    valid_ref,
    out,
    own,
    past,
    fresh,
    mixed,
    bias_ref,
    cache_send,
    cache_recv,
    fresh_send,
    fresh_recv,
    out_send,
    out_recv,
    hop_send,
    hop_recv,
    cache_keep,
    fresh_keep,
    out_keep,
):
    c, last = lax.axis_index("tm"), lax.axis_size("tm") - 1
    s, space = lax.axis_index("space"), lax.axis_size("space")
    cache_in, fresh_in = (ck_in, cv_in), (q_in, k_in, v_in)
    tokens = q_in.shape[1]
    heads, stretch_len = own.shape[1], own.shape[2]
    some = heads // groups
    has_next = c < last
    hops = WIN - 1

    def part(g):
        return pl.ds(g * some, some)

    def held_by(p, g):
        return pl.ds(p * heads + g * some, some)

    def tokens_of(p):
        return pl.ds(pl.multiple_of(p * tokens, tokens), tokens)

    def spread(sources, dst, send, recv, keep, g):
        remote, local = [], []
        for kind, src in enumerate(sources):
            landing = dst.at[kind, part(g), tokens_of(s)]
            for apart in range(1, space):
                p = lax.rem(s + apart, space)
                remote.append(
                    pltpu.make_async_remote_copy(
                        src_ref=src.at[held_by(p, g)],
                        dst_ref=landing,
                        send_sem=send.at[kind, g, apart - 1],
                        recv_sem=recv.at[kind, g, apart - 1],
                        device_id={"space": p},
                        device_id_type=MESH,
                    )
                )
            local.append(pltpu.make_async_copy(src.at[held_by(s, g)], landing, keep.at[kind, g]))
        return remote, local

    def cache_copies(g):
        return spread(cache_in, own, cache_send, cache_recv, cache_keep, g)

    def fresh_copies(g):
        return spread(fresh_in, fresh, fresh_send, fresh_recv, fresh_keep, g)

    def out_copies(g):
        remote = []
        for apart in range(1, space):
            p = lax.rem(s + apart, space)
            remote.append(
                pltpu.make_async_remote_copy(
                    src_ref=mixed.at[part(g), tokens_of(p)],
                    dst_ref=out.at[held_by(s, g)],
                    send_sem=out_send.at[g, apart - 1],
                    recv_sem=out_recv.at[g, apart - 1],
                    device_id={"space": p},
                    device_id_type=MESH,
                )
            )
        local = pltpu.make_async_copy(
            mixed.at[part(g), tokens_of(s)], out.at[held_by(s, g)], out_keep.at[g]
        )
        return remote, [local]

    def start(copies):
        remote, local = copies
        for copy in remote + local:
            copy.start()

    def arrive(copies):
        remote, local = copies
        for copy in remote:
            copy.wait_recv()
        for copy in local:
            copy.wait()

    def hop(j, g):
        return pltpu.make_async_remote_copy(
            src_ref=own.at[:, part(g)] if j == 0 else past.at[j - 1, :, part(g)],
            dst_ref=past.at[j, :, part(g)],
            send_sem=hop_send.at[j, g],
            recv_sem=hop_recv.at[j, g],
            device_id={"tm": c + 1},
            device_id_type=MESH,
        )

    barrier = pltpu.get_barrier_semaphore()
    for apart in range(1, space):
        pl.semaphore_signal(
            barrier,
            inc=1,
            device_id={"space": lax.rem(s + apart, space)},
            device_id_type=MESH,
        )

    @pl.when(has_next)
    def _():
        pl.semaphore_signal(barrier, inc=1, device_id={"tm": c + 1}, device_id_type=MESH)

    @pl.when(c > 0)
    def _():
        pl.semaphore_signal(barrier, inc=1, device_id={"tm": c - 1}, device_id_type=MESH)

    pl.semaphore_wait(
        barrier, space - 1 + jnp.where(has_next, 1, 0) + jnp.where(c > 0, 1, 0)
    )

    @pl.when(has_next)
    def _():
        start(cache_copies(0))
        if groups > 1:
            start(cache_copies(1))

    def see(a, carry):
        column = lax.broadcasted_iota(jnp.int32, (1, WIN * stretch_len), 1)
        seen = column < 0
        for slot in range(list_ref.shape[1]):
            first = jnp.where(slot < count_ref[a], list_ref[a, slot] * BLOCK, -BLOCK)
            seen = seen | ((column >= first) & (column < first + BLOCK))
        live = column < 0
        for o in range(WIN):
            source = c - hops + o
            length = jnp.where(source >= 0, valid_ref[jnp.maximum(source, 0)], 0)
            live = live | ((column >= o * stretch_len) & (column < o * stretch_len + length))
        bias_ref[a] = jnp.where(seen & live, 0.0, NEG)
        return carry

    lax.fori_loop(0, stretch_len // BLOCK, see, 0)

    for j in range(hops):

        @pl.when(c <= j)
        def _(j=j):
            def clear(h, carry):
                for kind in range(2):
                    past[j, kind, h] = jnp.zeros(past.shape[3:], past.dtype)
                return carry

            lax.fori_loop(0, heads, clear, 0)

    @pl.when(has_next)
    def _():
        arrive(cache_copies(0))
        hop(0, 0).start()

    start(fresh_copies(0))

    def attend_head(h):
        blocks = rows // BLOCK
        k_parts = [past.at[hops - 1 - o, 0, h] for o in range(hops)] + [fresh.at[1, h]]
        v_parts = [past.at[hops - 1 - o, 1, h] for o in range(hops)] + [fresh.at[2, h]]

        def step(i, carry):
            at = pl.multiple_of(i * rows, rows)
            mixed[h, pl.ds(at, rows)] = attend(
                fresh[0, h, pl.ds(at, rows)],
                [k[...] for k in k_parts],
                [v[...] for v in v_parts],
                bias_ref[pl.ds(i * blocks, blocks)],
                lax.broadcasted_iota(jnp.int32, (rows, 1), 0) + at < valid_ref[c],
                fold,
            )
            return carry

        lax.fori_loop(0, stretch_len // rows, step, 0)

    def turn(g, carry):
        @pl.when((g + 2 < groups) & has_next)
        def _():
            start(cache_copies(g + 2))

        @pl.when(g + 1 < groups)
        def _():
            start(fresh_copies(g + 1))

        for j in range(hops - 1):

            @pl.when((g < groups) & (c >= j + 1))
            def _(j=j):
                hop(j, g).wait_recv()

            @pl.when((g < groups) & (c >= j + 1) & has_next)
            def _(j=j):
                hop(j + 1, g).start()

        @pl.when((g + 1 < groups) & has_next)
        def _():
            arrive(cache_copies(g + 1))
            hop(0, g + 1).start()

        @pl.when(g > 0)
        def _():
            done = g - 1

            @pl.when(c >= hops)
            def _():
                hop(hops - 1, done).wait_recv()

            arrive(fresh_copies(done))

            def one(i, carry):
                attend_head(done * some + i)
                return carry

            lax.fori_loop(0, some, one, 0)
            start(out_copies(done))

        return carry

    lax.fori_loop(0, groups + 1, turn, 0)

    def finish(g, carry):
        @pl.when(has_next)
        def _():
            for copy in cache_copies(g)[0]:
                copy.wait_send()

        for copy in fresh_copies(g)[0]:
            copy.wait_send()
        for j in range(hops):

            @pl.when(has_next & (c >= j))
            def _(j=j):
                hop(j, g).wait_send()

        remote, local = out_copies(g)
        for copy in remote + local:
            copy.wait()
        return carry

    lax.fori_loop(0, groups, finish, 0)


def exchange_and_attend(cache, fresh, block_list, block_count, valid_tokens):
    space = lax.axis_size("space")
    all_heads, tokens, d = fresh[0].shape
    dtype = fresh[0].dtype
    heads, stretch_len = all_heads // space, tokens * space
    groups = max(n for n in range(1, GROUPS + 1) if heads % n == 0)
    fold = math.log2(math.e) / math.sqrt(d)
    rows = rows_at_once(stretch_len)
    dma = pltpu.SemaphoreType.DMA
    return pl.pallas_call(
        functools.partial(exchange_kernel, fold, rows, groups),
        out_shape=jax.ShapeDtypeStruct((all_heads, tokens, d), dtype),
        in_specs=[pl.BlockSpec(memory_space=pl.ANY)] * 5
        + [pl.BlockSpec(memory_space=pltpu.SMEM)] * 3,
        out_specs=pl.BlockSpec(memory_space=pl.ANY),
        scratch_shapes=[
            pltpu.VMEM((2, heads, stretch_len, d), dtype),
            pltpu.VMEM((WIN - 1, 2, heads, stretch_len, d), dtype),
            pltpu.VMEM((3, heads, stretch_len, d), dtype),
            pltpu.VMEM((heads, stretch_len, d), dtype),
            pltpu.VMEM((stretch_len // BLOCK, 1, WIN * stretch_len), jnp.float32),
        ]
        + [dma((2, groups, space - 1))] * 2
        + [dma((3, groups, space - 1))] * 2
        + [dma((groups, space - 1))] * 2
        + [dma((WIN - 1, groups))] * 2
        + [dma((2, groups)), dma((3, groups)), dma((groups,))],
        compiler_params=pltpu.CompilerParams(
            collective_id=0, has_side_effects=True, vmem_limit_bytes=50 * 1024 * 1024
        ),
        cost_estimate=pl.CostEstimate(
            flops=4 * heads * stretch_len * WIN * stretch_len * d,
            bytes_accessed=12 * heads * stretch_len * d,
            transcendentals=heads * stretch_len * WIN * stretch_len,
        ),
    )(*cache, *fresh, block_list, block_count, valid_tokens)


def on_device(
    queries,
    noisy_keys,
    noisy_values,
    cache_keys,
    cache_values,
    block_list,
    block_count,
    valid_tokens,
):
    def by_heads(x):
        return jnp.transpose(x[0], (1, 0, 2))

    back = exchange_and_attend(
        (by_heads(cache_keys), by_heads(cache_values)),
        (by_heads(queries), by_heads(noisy_keys), by_heads(noisy_values)),
        block_list[0],
        block_count[0],
        valid_tokens,
    )
    return jnp.transpose(back, (1, 0, 2))[None]


def solution(mesh):
    placed = (
        P("tm", "space", None, None),
        P("tm", "space", None, None),
        P("tm", "space", None, None),
        P("tm", "space", None, None),
        P("tm", "space", None, None),
        P("tm", None, None),
        P("tm", None),
        P(),
    )
    return jax.shard_map(
        on_device,
        mesh=mesh,
        in_specs=placed,
        out_specs=P("tm", "space", None, None),
        check_vma=False,
    )
```
